32 devices in a mesh: section: 4 (over z), ep: 8 (over y, x, core).
Axes of the slice: x: 2, y: 2, z: 4, core: 2. Of those that a mesh axis runs over, the one named last changes fastest.
Arguments:
- fresh_tokens: bfloat16 [128, 3584], P('ep'), may hold values from -6 to 6
- sent_forward: bfloat16 [4, 128, 3584], P('section', 'ep'), may hold values from -6 to 6
- sent_backward: bfloat16 [4, 128, 3584], P('section', 'ep'), may hold values from -1.1953125 to 1.1953125
- turn_gradient: bfloat16 [128, 3584], P('ep'), may hold values from -1.1953125 to 1.1953125
- saved_input: bfloat16 [4, 128, 3584], P('section', 'ep'), may hold values from -6 to 6
- gain: bfloat16 [4, 3584], P('section'), may hold values from 0.5 to 1.5
- ids_front: int32 [4, 128, 2], P('section', 'ep'), may hold values from 0 to 7, all different within a row; in each aligned block of 16 rows (0 to 15, 16 to 31, ..., all dimensions but the last counted through in order) at most 8 rows name the same one
- affinity_front: float32 [4, 128, 2], P('section', 'ep'), may hold values from 0.1 to 1
- ids_back: int32 [4, 128, 2], P('section', 'ep'), may hold values from 0 to 7, all different within a row; in each aligned block of 16 rows (0 to 15, 16 to 31, ..., all dimensions but the last counted through in order) at most 8 rows name the same one
- affinity_back: float32 [4, 128, 2], P('section', 'ep'), may hold values from 0.1 to 1
- w_gate: bfloat16 [4, 3584, 8192], P('section', None, 'ep'), may hold values from -0.09375 to 0.09375
- w_up: bfloat16 [4, 3584, 8192], P('section', None, 'ep'), may hold values from -0.09375 to 0.09375
- w_down: bfloat16 [4, 8192, 3584], P('section', 'ep'), may hold values from -0.1875 to 0.1875
- mirror_gate: bfloat16 [4, 3584, 8192], P('section', None, 'ep'), may hold values from -6 to 6
- mirror_up: bfloat16 [4, 3584, 8192], P('section', None, 'ep'), may hold values from -6 to 6
- mirror_down: bfloat16 [4, 8192, 3584], P('section', 'ep'), may hold values from -6 to 6
Outputs:
- forward_out: bfloat16 [4, 128, 3584], P('section', 'ep')
- grad_input: bfloat16 [4, 128, 3584], P('section', 'ep')
- grad_gate: bfloat16 [4, 3584, 8192], P('section', None, 'ep')
- grad_up: bfloat16 [4, 3584, 8192], P('section', None, 'ep')
- grad_down: bfloat16 [4, 8192, 3584], P('section', 'ep')
The draws below stay inside these ranges and needn't reach their ends.
Inputs may be any that keep to these rules, and one draw needn't show every extreme that they name: `ids_front`: each row names 2 different experts. In each aligned block of 16 rows (the rows of one device) no expert is named by more than 8 rows, a bound that some block reaches. `ids_back`: each row names 2 different experts. In each aligned block of 16 rows (the rows of one device) no expert is named by more than 8 rows, a bound that some block reaches.
All inputs are finite; a program needn't handle non-finite values.
Results may differ from the reference program's by a relative error of at most 0.0068.
Values may be sent and summed in bfloat16 or wider, within the bound.
No kernel may reach another device: no remote copies, remote signals or barrier semaphores. Data moves between devices by JAX's collectives and lax.ppermute only.
A program may use at most 128 MiB of HBM per device.

```python
import math
import jax
import jax.numpy as jnp
import numpy as np
from jax import lax

D = 3584
H = 1024
EXPERTS = 8
TOP = 2
TOK = 16
GROUP = 1
SLICE = 1024
CAP = 8
TOKENS = 128
UNITS = 8192
N_SECTION = 4
N_EP = 8


def levels(stream_key, dims, pieces, smallest, largest):
    factor_of, own = 1.0, jax.random.fold_in(stream_key, 6)
    for dim, blocks in pieces:
        heights = jnp.exp(jax.random.uniform(jax.random.fold_in(own, dim), (blocks,), jnp.float32, smallest / len(pieces), largest / len(pieces)))
        factor_of = factor_of * jnp.repeat(heights, dims[dim] // blocks).reshape([-1 if axis == dim else 1 for axis in range(len(dims))])
    return factor_of


def shared_out(key, own, number, rows, number_of, top, bound, skew):
    ranking = jax.random.permutation(key, number_of)
    crowded, ordinary = load_shares(number_of, rows * top, bound, skew, True), load_shares(number_of, rows * top, bound, skew, False)
    places = jnp.arange(number_of)

    def named(lengths, rotation):
        used = int((lengths > 0).sum())
        fixed = max(1, used // 4)
        shifted = fixed + (places - fixed + rotation * (used - fixed)) % max(1, number_of - fixed)
        return jnp.zeros((number_of,), jnp.int32).at[ranking[jnp.where(places < fixed, places, shifted)]].set(jnp.asarray(lengths, jnp.int32))

    lengths = jnp.where(number % 4 == 0, named(crowded, number // 4), named(ordinary, number - number // 4 - 1))
    mixed = jax.random.permutation(jax.random.fold_in(own, 3), number_of)
    source_of, sink = mixed[0:number_of // 2 * 2:2], mixed[1:number_of // 2 * 2:2]
    room = jnp.minimum(lengths[source_of] - 1, bound - lengths[sink]) // 2
    room = jnp.where((source_of == ranking[0]) | (sink == ranking[0]) | (lengths[sink] == 0), 0, jnp.maximum(room, 0))
    shifted = jax.random.randint(jax.random.fold_in(own, 4), (number_of // 2,), 0, 1 << 20) % (room + 1)
    lengths = lengths.at[source_of].add(-shifted).at[sink].add(shifted)
    items = jnp.searchsorted(jnp.cumsum(lengths), jnp.arange(rows * top), side="right").astype(jnp.int32)
    grid = items.reshape(top, rows).T
    grid = grid[jax.random.permutation(jax.random.fold_in(own, 1), rows)]
    rotation = jax.random.randint(jax.random.fold_in(own, 2), (rows, 1), 0, top)
    return jnp.take_along_axis(grid, (jnp.arange(top)[None, :] + rotation) % top, axis=1)


def load_shares(number_of, total, most, lean, full):
    loads = [(1 << 20) // math.isqrt(rank ** lean) + 1 for rank in range(1, number_of + 1)]
    largest = most if full else min(most, max(-(-total // number_of), total * loads[0] // sum(loads)))
    least = 1 if total - largest >= number_of - 1 else 0
    given, spare = [largest] + [least] * (number_of - 1), total - largest - least * (number_of - 1)
    while spare > 0:
        free = [i for i in range(1, number_of) if given[i] < largest] or [i for i in range(1, number_of) if given[i] < most]
        mass, budget = sum([loads[i] for i in free]), spare
        for i in free:
            extra = min(most - given[i], max(1, budget * loads[i] // mass), spare)
            given[i] = given[i] + extra
            spare = spare - extra
    return np.array(given)


def normal_values(stream_key, shape, width, bound, shards=(), kind=jnp.bfloat16):
    level = levels(stream_key, shape, shards, -0.22, 0.18) if shards else 1.0
    drawn = jax.random.normal(stream_key, shape, jnp.float32) * width * level
    return jnp.minimum(jnp.maximum(drawn, -bound), bound).astype(kind)


def setup_inputs(seed: int = 0) -> dict:
    streams_of = jax.random.split(jax.random.key(seed), 17)
    fresh_tokens = normal_values(streams_of[0], (TOKENS, D), 1.0, 6.0, ((0, 8),))
    sent_forward = normal_values(streams_of[1], (N_SECTION, TOKENS, D), 1.0, 6.0, ((0, 4), (1, 8)))
    sent_backward = normal_values(streams_of[2], (N_SECTION, TOKENS, D), 0.2, 1.1953125, ((0, 4), (1, 8)))
    turn_gradient = normal_values(streams_of[3], (TOKENS, D), 0.2, 1.1953125, ((0, 8),))
    saved_input = normal_values(streams_of[4], (N_SECTION, TOKENS, D), 1.0, 6.0, ((0, 4), (1, 8)))
    gain = jnp.clip(1.0 + 0.1 * jax.random.normal(streams_of[5], (N_SECTION, D), jnp.float32), 0.5, 1.5).astype(jnp.bfloat16)
    ids_front_keys = jax.random.split(jax.random.fold_in(streams_of[6], 1), N_SECTION * TOKENS // TOK)
    ids_front_turns = jax.random.permutation(jax.random.fold_in(streams_of[6], 3), N_SECTION * TOKENS // TOK)
    ids_front = jax.vmap(lambda own, number: shared_out(jax.random.fold_in(streams_of[6], 2), own, number, TOK, EXPERTS, TOP, CAP, 2))(ids_front_keys, ids_front_turns).reshape((N_SECTION, TOKENS, TOP))
    affinity_front = jnp.clip(jnp.exp(math.log(1.0) - 2.3025851 * jax.random.uniform(streams_of[7], (N_SECTION, TOKENS, TOP), jnp.float32) ** levels(streams_of[7], (N_SECTION, TOKENS, TOP), ((0, 4), (1, 8)), -0.2, 0.2)), 0.1, 1.0)
    ids_back_keys = jax.random.split(jax.random.fold_in(streams_of[8], 1), N_SECTION * TOKENS // TOK)
    ids_back_turns = jax.random.permutation(jax.random.fold_in(streams_of[8], 3), N_SECTION * TOKENS // TOK)
    ids_back = jax.vmap(lambda own, number: shared_out(jax.random.fold_in(streams_of[8], 2), own, number, TOK, EXPERTS, TOP, CAP, 2))(ids_back_keys, ids_back_turns).reshape((N_SECTION, TOKENS, TOP))
    affinity_back = jnp.clip(jnp.exp(math.log(1.0) - 2.3025851 * jax.random.uniform(streams_of[9], (N_SECTION, TOKENS, TOP), jnp.float32) ** levels(streams_of[9], (N_SECTION, TOKENS, TOP), ((0, 4), (1, 8)), -0.2, 0.2)), 0.1, 1.0)
    w_gate = normal_values(streams_of[10], (N_SECTION, D, UNITS), D ** -0.5, 0.09375, ((0, 4), (2, 8)))
    w_up = normal_values(streams_of[11], (N_SECTION, D, UNITS), D ** -0.5, 0.09375, ((0, 4), (2, 8)))
    w_down = normal_values(streams_of[12], (N_SECTION, UNITS, D), H ** -0.5, 0.1875, ((0, 4), (1, 8)))
    mirror_gate = normal_values(streams_of[13], (N_SECTION, D, UNITS), 1.0, 6.0, ((0, 4), (2, 8)))
    mirror_up = normal_values(streams_of[14], (N_SECTION, D, UNITS), 1.0, 6.0, ((0, 4), (2, 8)))
    mirror_down = normal_values(streams_of[15], (N_SECTION, UNITS, D), 1.0, 6.0, ((0, 4), (1, 8)))
    return {"fresh_tokens": fresh_tokens, "sent_forward": sent_forward, "sent_backward": sent_backward, "turn_gradient": turn_gradient, "saved_input": saved_input, "gain": gain, "ids_front": ids_front, "affinity_front": affinity_front, "ids_back": ids_back, "affinity_back": affinity_back, "w_gate": w_gate, "w_up": w_up, "w_down": w_down, "mirror_gate": mirror_gate, "mirror_up": mirror_up, "mirror_down": mirror_down}


highest = lax.Precision.HIGHEST

def silu_of(pre_act):
    return pre_act * jax.nn.sigmoid(pre_act)

def rounded(values):
    return lax.optimization_barrier(values.astype(jnp.bfloat16)).astype(jnp.float32)

def norm_rows(inputs, gain):
    values = inputs.astype(jnp.float32)
    inverse = lax.rsqrt(lax.optimization_barrier(jnp.mean(values * values, axis=-1, keepdims=True)) + 1e-06)
    normed = (values * inverse * gain.astype(jnp.float32)).astype(jnp.bfloat16)
    return (values, inverse, normed)

def slot_tables(route_ids, affinity, capacity):
    flat_ids = route_ids.reshape(-1)
    onehot = (flat_ids[:, None] == jnp.arange(EXPERTS, dtype=jnp.int32)[None, :]).astype(jnp.int32)
    earlier = jnp.cumsum(onehot, axis=0) - onehot
    position = lax.optimization_barrier(jnp.sum(earlier * onehot, axis=1))
    target = (flat_ids * capacity + position).reshape(route_ids.shape)
    columns = jnp.arange(EXPERTS * capacity, dtype=jnp.int32)
    matches = (target[:, :, None] == columns[None, None, :]).astype(jnp.float32)
    shares = affinity / lax.optimization_barrier(jnp.sum(affinity, axis=1, keepdims=True))
    return (lax.optimization_barrier(jnp.sum(matches, axis=1)), lax.optimization_barrier(jnp.sum(matches * shares[:, :, None], axis=1)))

def route_tables(route_ids, affinity):

    def one_block(ids_block, aff_block):
        return slot_tables(ids_block, aff_block, CAP)
    return jax.vmap(one_block)(route_ids.reshape(N_EP, TOK, TOP), affinity.reshape(N_EP, TOK, TOP))

def expert_forward(token_rows, gate_cols, up_cols, down_rows):
    gate_pre = jnp.dot(token_rows, gate_cols, preferred_element_type=jnp.float32)
    up_pre = jnp.dot(token_rows, up_cols, preferred_element_type=jnp.float32)
    hidden = (silu_of(gate_pre) * up_pre).astype(jnp.bfloat16)
    total = jnp.zeros((token_rows.shape[0], D), jnp.float32)
    for piece in range(GROUP):
        part_cols = slice(piece * SLICE, (piece + 1) * SLICE)
        total = total + rounded(jnp.dot(hidden[:, part_cols], down_rows[part_cols], preferred_element_type=jnp.float32))
    return total

def expert_backward(token_rows, grad_rows, gate_cols, up_cols, down_rows):
    gate_pre = jnp.dot(token_rows, gate_cols, preferred_element_type=jnp.float32)
    up_pre = jnp.dot(token_rows, up_cols, preferred_element_type=jnp.float32)
    gate_sig = jax.nn.sigmoid(gate_pre)
    active = gate_pre * gate_sig
    hidden = (active * up_pre).astype(jnp.bfloat16)
    grad_hidden = jnp.dot(grad_rows, down_rows.T, preferred_element_type=jnp.float32)
    grad_down = jnp.dot(hidden.T, grad_rows, preferred_element_type=jnp.float32)
    grad_gate_pre = (grad_hidden * up_pre * gate_sig * (1.0 + gate_pre * (1.0 - gate_sig))).astype(jnp.bfloat16)
    grad_up_pre = (grad_hidden * active).astype(jnp.bfloat16)
    grad_gate = jnp.dot(token_rows.T, grad_gate_pre, preferred_element_type=jnp.float32)
    grad_up = jnp.dot(token_rows.T, grad_up_pre, preferred_element_type=jnp.float32)
    total = jnp.zeros((token_rows.shape[0], D), jnp.float32)
    for piece in range(GROUP):
        part_cols = slice(piece * SLICE, (piece + 1) * SLICE)
        term = jnp.dot(grad_gate_pre[:, part_cols], gate_cols[:, part_cols].T, preferred_element_type=jnp.float32)
        term = term + jnp.dot(grad_up_pre[:, part_cols], up_cols[:, part_cols].T, preferred_element_type=jnp.float32)
        total = total + rounded(term)
    return (grad_gate, grad_up, grad_down, total)

def pack_rows(member, normed):
    packed = jnp.einsum('btm,btd->bmd', member, normed.astype(jnp.float32))
    return packed.astype(jnp.bfloat16).reshape(N_EP, EXPERTS, CAP, D)

def forward_section(inputs, gain, route_ids, affinity, w_gate, w_up, w_down):
    values, inverse, normed = norm_rows(inputs.reshape(N_EP, TOK, D), gain)
    member, weighted = route_tables(route_ids, affinity)
    packed = pack_rows(member, normed)
    outputs = []
    for expert in range(EXPERTS):
        cols = slice(expert * H, (expert + 1) * H)
        token_rows = packed[:, expert].reshape(N_EP * CAP, D)
        outputs.append(expert_forward(token_rows, w_gate[:, cols], w_up[:, cols], w_down[cols]).reshape(N_EP, CAP, D))
    totals = jnp.stack(outputs, axis=1).reshape(N_EP, EXPERTS * CAP, D)
    mixed = values + jnp.einsum('btm,bmd->btd', weighted, totals, precision=highest)
    return mixed.astype(jnp.bfloat16).reshape(TOKENS, D)

def backward_section(saved, cotangent, gain, route_ids, affinity, w_gate, w_up, w_down, mirror_gate, mirror_up, mirror_down):
    values, inverse, normed = norm_rows(saved.reshape(N_EP, TOK, D), gain)
    member, weighted = route_tables(route_ids, affinity)
    upstream = cotangent.reshape(N_EP, TOK, D).astype(jnp.float32)
    packed = pack_rows(member, normed)
    grad_packed = jnp.einsum('btm,btd->bmd', weighted, upstream, precision=highest)
    grad_packed = grad_packed.astype(jnp.bfloat16).reshape(N_EP, EXPERTS, CAP, D)
    gate_list, up_list, down_list, slot_list = ([], [], [], [])
    for expert in range(EXPERTS):
        cols = slice(expert * H, (expert + 1) * H)
        token_rows = packed[:, expert].reshape(N_EP * CAP, D)
        grad_rows = grad_packed[:, expert].reshape(N_EP * CAP, D)
        g_gate, g_up, g_down, total = expert_backward(token_rows, grad_rows, w_gate[:, cols], w_up[:, cols], w_down[cols])
        gate_list.append(g_gate)
        up_list.append(g_up)
        down_list.append(g_down)
        slot_list.append(total.reshape(N_EP, CAP, D))
    grad_gate = (mirror_gate.astype(jnp.float32) + jnp.concatenate(gate_list, axis=1)).astype(jnp.bfloat16)
    grad_up = (mirror_up.astype(jnp.float32) + jnp.concatenate(up_list, axis=1)).astype(jnp.bfloat16)
    grad_down = (mirror_down.astype(jnp.float32) + jnp.concatenate(down_list, axis=0)).astype(jnp.bfloat16)
    totals = jnp.stack(slot_list, axis=1).reshape(N_EP, EXPERTS * CAP, D)
    grad_normed = jnp.einsum('btm,bmd->btd', member, totals, precision=highest)
    scaled = grad_normed * gain.astype(jnp.float32)
    cubed = inverse * inverse * inverse
    grad_inputs = upstream + inverse * scaled - cubed * values * lax.optimization_barrier(jnp.mean(scaled * values, axis=-1, keepdims=True))
    return (grad_inputs.astype(jnp.bfloat16).reshape(TOKENS, D), grad_gate, grad_up, grad_down)

def reference(fresh_tokens, sent_forward, sent_backward, turn_gradient, saved_input, gain, ids_front, affinity_front, ids_back, affinity_back, w_gate, w_up, w_down, mirror_gate, mirror_up, mirror_down):
    forward_list, input_list, gate_list, up_list, down_list = ([], [], [], [], [])
    for section_id in range(N_SECTION):
        front_in = fresh_tokens if section_id == 0 else sent_forward[section_id - 1]
        upstream_in = turn_gradient if section_id == N_SECTION - 1 else sent_backward[section_id + 1]
        forward_list.append(forward_section(front_in, gain[section_id], ids_front[section_id], affinity_front[section_id], w_gate[section_id], w_up[section_id], w_down[section_id]))
        grad_inputs, grad_gate, grad_up, grad_down = backward_section(saved_input[section_id], upstream_in, gain[section_id], ids_back[section_id], affinity_back[section_id], w_gate[section_id], w_up[section_id], w_down[section_id], mirror_gate[section_id], mirror_up[section_id], mirror_down[section_id])
        input_list.append(grad_inputs)
        gate_list.append(grad_gate)
        up_list.append(grad_up)
        down_list.append(grad_down)
    return (jnp.stack(forward_list), jnp.stack(input_list), jnp.stack(gate_list), jnp.stack(up_list), jnp.stack(down_list))
```

```python
import functools

import jax
import jax.numpy as jnp
from jax import lax
from jax.experimental import pallas as pl
from jax.experimental.pallas import tpu as pltpu
from jax.sharding import PartitionSpec as P

EXPERTS = 8
F32 = jnp.float32
BF16 = jnp.bfloat16
MIB = 1 << 20


def dot_nn(a, b):
    return jnp.dot(a, b, preferred_element_type=F32)


def dot_nt(a, b):
    return lax.dot_general(a, b, (((1,), (1,)), ((), ())), preferred_element_type=F32)


def dot_tn(a, b):
    return lax.dot_general(a, b, (((0,), (0,)), ((), ())), preferred_element_type=F32)


def norm_rows(values, gain):
    inverse = lax.rsqrt(jnp.mean(values * values, axis=-1, keepdims=True) + 1e-06)
    return inverse, (values * inverse * gain).astype(BF16)


def choice_tables(ids, capacity, groups):
    tokens = ids.shape[0]
    columns = EXPERTS * groups * capacity
    column = lax.broadcasted_iota(jnp.int32, (tokens, columns), 1)
    expert = column // (groups * capacity)
    slot = (column % capacity).astype(F32)
    named = [(ids[:, j : j + 1] == expert).astype(F32) for j in range(2)]
    row = lax.broadcasted_iota(jnp.int32, (tokens, tokens), 0)
    col = lax.broadcasted_iota(jnp.int32, (tokens, tokens), 1)
    earlier = dot_nn((col < row).astype(BF16), (named[0] + named[1]).astype(BF16))
    here = (earlier == slot).astype(F32)
    return [(n * here).astype(BF16) for n in named]


def shares_of(affinity):
    total = affinity[:, 0:1] + affinity[:, 1:2]
    return affinity[:, 0:1] / total, affinity[:, 1:2] / total


def pack_kernel(
    capacity,
    groups,
    place_ref,
    arrived_ref,
    fresh_ref,
    returned_ref,
    turn_ref,
    saved_ref,
    gain_ref,
    ids_front_ref,
    ids_back_ref,
    aff_back_ref,
    packed_ref,
    front_ref,
    upstream_ref,
):
    width = fresh_ref.shape[1]
    gain = gain_ref[...].astype(F32)
    front = jnp.where(place_ref[0] == 0, fresh_ref[...].astype(F32), arrived_ref[...].astype(F32))
    upstream = jnp.where(
        place_ref[1] == 0, turn_ref[...].astype(F32), returned_ref[...].astype(F32)
    )
    front_ref[...] = front.astype(BF16)
    upstream_ref[...] = upstream.astype(BF16)
    _, normed = norm_rows(front, gain)
    first, second = choice_tables(ids_front_ref[...], capacity, groups)
    packed_ref[:, :width] = dot_tn(first + second, normed).astype(BF16)
    _, normed = norm_rows(saved_ref[...].astype(F32), gain)
    first, second = choice_tables(ids_back_ref[...], capacity, groups)
    packed_ref[:, width : 2 * width] = dot_tn(first + second, normed).astype(BF16)
    shares = shares_of(aff_back_ref[...])
    packed_ref[:, 2 * width :] = (
        dot_tn(first, (shares[0] * upstream).astype(BF16))
        + dot_tn(second, (shares[1] * upstream).astype(BF16))
    ).astype(BF16)


def expert_kernel(
    rows_ref, gate_ref, up_ref, down_ref, parts_ref, rows_t_ref, hidden_t_ref, dgate_ref, dup_ref, both_ref, front_acc, back_acc
):
    step = pl.program_id(0)
    count = rows_ref.shape[0]
    width = gate_ref.shape[0]

    @pl.when(step == 0)
    def _():
        both_ref[:count] = rows_ref[:, :width]
        both_ref[count:] = rows_ref[:, width : 2 * width]
        rows_t_ref[...] = rows_ref[:, width : 2 * width].T
        front_acc[...] = jnp.zeros_like(front_acc)
        back_acc[...] = jnp.zeros_like(back_acc)

    both = both_ref[...]
    gate_pre = dot_nn(both, gate_ref[...])
    up_pre = dot_nn(both, up_ref[...])
    sig = jax.nn.sigmoid(gate_pre)
    active = gate_pre * sig
    hidden = (active * up_pre).astype(BF16)
    front_acc[...] += dot_nn(hidden[:count], down_ref[...])
    grad_hidden = dot_nt(rows_ref[:, 2 * width :], down_ref[...])
    back = slice(count, 2 * count)
    dgate = (grad_hidden * up_pre[back] * sig[back] * (1.0 + gate_pre[back] * (1.0 - sig[back]))).astype(BF16)
    dup = (grad_hidden * active[back]).astype(BF16)
    back_acc[...] += dot_nt(dgate, gate_ref[...]) + dot_nt(dup, up_ref[...])
    hidden_t_ref[...] = hidden[back].T
    dgate_ref[...] = dgate
    dup_ref[...] = dup

    @pl.when(step == pl.num_programs(0) - 1)
    def _():
        parts_ref[:, :width] = front_acc[...].astype(BF16)
        parts_ref[:, width:] = back_acc[...].astype(BF16)


def grads_kernel(
    rows_t_ref, hidden_t_ref, dgate_ref, dup_ref, grads_ref, mgate_ref, mup_ref, mdown_ref, ogate_ref, oup_ref, odown_ref
):
    rows_t = rows_t_ref[...]
    ogate_ref[...] = (mgate_ref[...].astype(F32) + dot_nn(rows_t, dgate_ref[...])).astype(BF16)
    oup_ref[...] = (mup_ref[...].astype(F32) + dot_nn(rows_t, dup_ref[...])).astype(BF16)
    odown_ref[...] = (mdown_ref[...].astype(F32) + dot_nn(hidden_t_ref[...], grads_ref[...])).astype(BF16)


def combine_kernel(
    capacity,
    groups,
    parts_ref,
    front_ref,
    upstream_ref,
    saved_ref,
    gain_ref,
    ids_front_ref,
    aff_front_ref,
    ids_back_ref,
    forward_ref,
    input_ref,
):
    width = front_ref.shape[1]
    first, second = choice_tables(ids_front_ref[...], capacity, groups)
    shares = shares_of(aff_front_ref[...])
    parts = parts_ref[:, :width]
    forward_ref[...] = (
        front_ref[...].astype(F32) + shares[0] * dot_nn(first, parts) + shares[1] * dot_nn(second, parts)
    ).astype(BF16)
    first, second = choice_tables(ids_back_ref[...], capacity, groups)
    gain = gain_ref[...].astype(F32)
    saved = saved_ref[...].astype(F32)
    inverse, _ = norm_rows(saved, gain)
    scaled = dot_nn(first + second, parts_ref[:, width:]) * gain
    cubed = inverse * inverse * inverse
    input_ref[...] = (
        upstream_ref[...].astype(F32)
        + inverse * scaled
        - cubed * saved * jnp.mean(scaled * saved, axis=-1, keepdims=True)
    ).astype(BF16)


def shape(dims, dtype=BF16):
    return jax.ShapeDtypeStruct(dims, dtype)


def whole(memory_space=pltpu.VMEM):
    return pl.BlockSpec(memory_space=memory_space)


def cost(flops, moved):
    return pl.CostEstimate(flops=int(flops), bytes_accessed=int(moved), transcendentals=0)


def exchanged(rows):
    return lax.all_to_all(rows, "ep", split_axis=0, concat_axis=0, tiled=True)


def ring(value, by):
    size = lax.axis_size("section")
    return lax.ppermute(value, "section", [(i, (i + by) % size) for i in range(size)])


def body(
    fresh_tokens,
    sent_forward,
    sent_backward,
    turn_gradient,
    saved_input,
    gain,
    ids_front,
    affinity_front,
    ids_back,
    affinity_back,
    w_gate,
    w_up,
    w_down,
    mirror_gate,
    mirror_up,
    mirror_down,
):
    peers = lax.axis_size("ep")
    groups = peers // EXPERTS
    tokens, width = fresh_tokens.shape
    capacity = max(groups, tokens * ids_front.shape[2] * 2 // EXPERTS)
    count = peers * capacity
    units = w_gate.shape[2]
    section_id = lax.axis_index("section")
    place = jnp.stack([section_id, lax.axis_size("section") - 1 - section_id]).astype(jnp.int32)
    returned = ring(sent_backward, -1)
    arrived = ring(sent_forward, 1)
    packed, front, upstream = pl.pallas_call(
        functools.partial(pack_kernel, capacity, groups),
        out_shape=(shape((count, 3 * width)), shape((tokens, width)), shape((tokens, width))),
        in_specs=[whole(pltpu.SMEM)] + [whole()] * 9,
        out_specs=(whole(),) * 3,
        compiler_params=pltpu.CompilerParams(vmem_limit_bytes=24 * MIB),
        cost_estimate=cost(2 * count * tokens * width * 4, 5 * count * width),
        name="pack_rows",
    )(
        place,
        arrived[0],
        fresh_tokens,
        returned[0],
        turn_gradient,
        saved_input[0],
        gain,
        ids_front[0],
        ids_back[0],
        affinity_back[0],
    )
    rows = exchanged(packed.reshape(peers, capacity, 3 * width)).reshape(count, 3 * width)
    chunk = min(256, units)
    parts, rows_t, hidden_t, dgate, dup = pl.pallas_call(
        expert_kernel,
        grid=(units // chunk,),
        out_shape=(
            shape((count, 2 * width)),
            shape((width, count)),
            shape((units, count)),
            shape((count, units)),
            shape((count, units)),
        ),
        in_specs=[
            pl.BlockSpec((count, 3 * width), lambda i: (0, 0)),
            pl.BlockSpec((width, chunk), lambda i: (0, i)),
            pl.BlockSpec((width, chunk), lambda i: (0, i)),
            pl.BlockSpec((chunk, width), lambda i: (i, 0)),
        ],
        out_specs=(
            pl.BlockSpec((count, 2 * width), lambda i: (0, 0)),
            pl.BlockSpec((width, count), lambda i: (0, 0)),
            pl.BlockSpec((chunk, count), lambda i: (i, 0)),
            pl.BlockSpec((count, chunk), lambda i: (0, i)),
            pl.BlockSpec((count, chunk), lambda i: (0, i)),
        ),
        scratch_shapes=[
            pltpu.VMEM((2 * count, width), BF16),
            pltpu.VMEM((count, width), F32),
            pltpu.VMEM((count, width), F32),
        ],
        compiler_params=pltpu.CompilerParams(vmem_limit_bytes=(28 if count <= 128 else 60) * MIB),
        cost_estimate=cost(2 * count * width * units * 8, 6 * width * units),
        name="expert_rows",
    )(rows, w_gate[0], w_up[0], w_down[0])
    back = exchanged(parts.reshape(peers, capacity, 2 * width)).reshape(count, 2 * width)
    steps = 8
    wide, deep = width // steps, units // steps
    grads = rows[:, 2 * width :]
    gate_spec = pl.BlockSpec((wide, units), lambda i: (i, 0))
    down_spec = pl.BlockSpec((deep, width), lambda i: (i, 0))
    out_gate, out_up, out_down = pl.pallas_call(
        grads_kernel,
        grid=(steps,),
        out_shape=(shape((width, units)), shape((width, units)), shape((units, width))),
        in_specs=[
            pl.BlockSpec((wide, count), lambda i: (i, 0)),
            pl.BlockSpec((deep, count), lambda i: (i, 0)),
            pl.BlockSpec((count, units), lambda i: (0, 0)),
            pl.BlockSpec((count, units), lambda i: (0, 0)),
            pl.BlockSpec((count, width), lambda i: (0, 2)),
            gate_spec,
            gate_spec,
            down_spec,
        ],
        out_specs=(gate_spec, gate_spec, down_spec),
        compiler_params=pltpu.CompilerParams(vmem_limit_bytes=24 * MIB),
        cost_estimate=cost(2 * count * width * units * 3, 12 * width * units),
        name="weight_grads",
    )(rows_t, hidden_t, dgate, dup, rows, mirror_gate[0], mirror_up[0], mirror_down[0])
    forward_out, grad_input = pl.pallas_call(
        functools.partial(combine_kernel, capacity, groups),
        out_shape=(shape((tokens, width)), shape((tokens, width))),
        in_specs=[whole()] * 8,
        out_specs=(whole(),) * 2,
        compiler_params=pltpu.CompilerParams(vmem_limit_bytes=24 * MIB),
        cost_estimate=cost(2 * count * tokens * width * 3, 4 * count * width),
        name="combine_rows",
    )(
        back,
        front,
        upstream,
        saved_input[0],
        gain,
        ids_front[0],
        affinity_front[0],
        ids_back[0],
    )
    return (forward_out[None], grad_input[None], out_gate[None], out_up[None], out_down[None])


def solution(mesh):
    return jax.shard_map(
        body,
        mesh=mesh,
        in_specs=(
            P("ep", None),
            P("section", "ep", None),
            P("section", "ep", None),
            P("ep", None),
            P("section", "ep", None),
            P("section", None),
            P("section", "ep", None),
            P("section", "ep", None),
            P("section", "ep", None),
            P("section", "ep", None),
            P("section", None, "ep"),
            P("section", None, "ep"),
            P("section", "ep", None),
            P("section", None, "ep"),
            P("section", None, "ep"),
            P("section", "ep", None),
        ),
        out_specs=(
            P("section", "ep", None),
            P("section", "ep", None),
            P("section", None, "ep"),
            P("section", None, "ep"),
            P("section", "ep", None),
        ),
        check_vma=False,
    )
```

```python
import functools

import jax
import jax.numpy as jnp
from jax import lax
from jax.experimental import pallas as pl
from jax.experimental.pallas import tpu as pltpu
from jax.sharding import PartitionSpec as P

EXPERTS = 8
F32 = jnp.float32
BF16 = jnp.bfloat16
MIB = 1 << 20


def dot_nn(a, b):
    return jnp.dot(a, b, preferred_element_type=F32)


def dot_nt(a, b):
    return lax.dot_general(a, b, (((1,), (1,)), ((), ())), preferred_element_type=F32)


def dot_tn(a, b):
    return lax.dot_general(a, b, (((0,), (0,)), ((), ())), preferred_element_type=F32)


def norm_rows(values, gain):
    inverse = lax.rsqrt(jnp.mean(values * values, axis=-1, keepdims=True) + 1e-06)
    return inverse, (values * inverse * gain).astype(BF16)


def choice_tables(ids, capacity, groups, flip):
    tokens = ids.shape[1]
    count = EXPERTS * groups * capacity
    row = lax.broadcasted_iota(jnp.int32, (count, tokens), 0)
    expert = ((row // capacity) ^ flip) // groups
    slot = (row % capacity).astype(F32)
    named = [(ids[j : j + 1, :] == expert).astype(F32) for j in range(2)]
    one = lax.broadcasted_iota(jnp.int32, (tokens, tokens), 0)
    other = lax.broadcasted_iota(jnp.int32, (tokens, tokens), 1)
    earlier = dot_nn((named[0] + named[1]).astype(BF16), (one < other).astype(BF16))
    here = (earlier == slot).astype(F32)
    return [n * here for n in named]


def shares_of(affinity):
    total = affinity[0:1, :] + affinity[1:2, :]
    return affinity[0:1, :] / total, affinity[1:2, :] / total


def as_column(row):
    size = row.shape[1]
    one = lax.broadcasted_iota(jnp.int32, (size, size), 0)
    other = lax.broadcasted_iota(jnp.int32, (size, size), 1)
    return jnp.sum(jnp.where(one == other, row, 0.0), axis=1, keepdims=True)


def early_kernel(
    capacity,
    groups,
    place_ref,
    fresh_hbm,
    turn_hbm,
    saved_hbm,
    gain_hbm,
    ids_front_hbm,
    aff_front_hbm,
    ids_back_hbm,
    aff_back_hbm,
    fresh_ref,
    turn_ref,
    saved_ref,
    gain_ref,
    rows_ref,
    front_table_ref,
    front_picks_ref,
    front_shares_ref,
    back_table_ref,
    back_picks_ref,
    slot_shares_ref,
    ids_front_ref,
    aff_front_ref,
    ids_back_ref,
    aff_back_ref,
    sems,
):
    pairs = (
        (ids_front_hbm, ids_front_ref),
        (aff_front_hbm, aff_front_ref),
        (ids_back_hbm, ids_back_ref),
        (aff_back_hbm, aff_back_ref),
        (saved_hbm, saved_ref),
        (gain_hbm, gain_ref),
        (fresh_hbm, fresh_ref),
        (turn_hbm, turn_ref),
    )
    copies = [pltpu.make_async_copy(*pair, sems.at[i]) for i, pair in enumerate(pairs)]
    for copy in copies:
        copy.start()
    for copy in copies[:4]:
        copy.wait()
    flip = place_ref[2]
    first, second = choice_tables(ids_front_ref[...], capacity, groups, flip)
    front_table_ref[...] = (first + second).astype(BF16)
    front_picks_ref[0] = first.T.astype(BF16)
    front_picks_ref[1] = second.T.astype(BF16)
    share = shares_of(aff_front_ref[...])
    front_shares_ref[0] = as_column(share[0])
    front_shares_ref[1] = as_column(share[1])
    first, second = choice_tables(ids_back_ref[...], capacity, groups, flip)
    both = first + second
    back_table_ref[...] = both.astype(BF16)
    back_picks_ref[...] = both.T.astype(BF16)
    share = shares_of(aff_back_ref[...])
    slot_shares_ref[...] = jnp.sum(first * share[0] + second * share[1], axis=1, keepdims=True)
    copies[4].wait()
    copies[5].wait()
    _, normed = norm_rows(saved_ref[...].astype(F32), gain_ref[...].astype(F32))
    rows_ref[...] = dot_nn(back_table_ref[...], normed).astype(BF16)
    copies[6].wait()
    copies[7].wait()


def pack_kernel(
    place_ref,
    arrived_ref,
    fresh_ref,
    returned_ref,
    turn_ref,
    gain_ref,
    rows_ref,
    front_table_ref,
    back_table_ref,
    slot_shares_ref,
    front_ref,
    upstream_ref,
    *packed_refs,
):
    width = fresh_ref.shape[1]
    front = jnp.where(place_ref[0] == 0, fresh_ref[...].astype(F32), arrived_ref[...].astype(F32))
    upstream = jnp.where(place_ref[1] == 0, turn_ref[...].astype(F32), returned_ref[...].astype(F32))
    front_ref[...] = front.astype(BF16)
    upstream_ref[...] = upstream.astype(BF16)
    _, normed = norm_rows(front, gain_ref[...].astype(F32))
    front_rows = dot_nn(front_table_ref[...], normed).astype(BF16)
    grad_rows = (slot_shares_ref[...] * dot_nn(back_table_ref[...], upstream.astype(BF16))).astype(BF16)
    back_rows = rows_ref[...]
    for i, packed_ref in enumerate(packed_refs):
        at = slice(i * packed_ref.shape[0], (i + 1) * packed_ref.shape[0])
        packed_ref[:, :width] = front_rows[at]
        packed_ref[:, width : 2 * width] = back_rows[at]
        packed_ref[:, 2 * width :] = grad_rows[at]


def load_kernel(amount, *refs):
    after, sources, targets, sems = refs[0], refs[1 : 1 + amount], refs[1 + amount : 1 + 2 * amount], refs[-1]
    del after
    copies = [pltpu.make_async_copy(a, b, sems.at[i]) for i, (a, b) in enumerate(zip(sources, targets))]
    for copy in copies:
        copy.start()
    for copy in copies:
        copy.wait()


def expert_kernel(
    chunk,
    tile,
    pieces,
    gate_ref,
    up_ref,
    down_ref,
    *refs,
):
    rows_refs, refs = refs[:pieces], refs[pieces:]
    grads_ref, rows_t_ref, hidden_t_ref, dgate_ref, dup_ref = refs[:5]
    parts_refs = refs[5 : 5 + pieces]
    both_ref, grads_t_ref, dgate_t_ref, dup_t_ref, front_ref = refs[5 + pieces :]
    width, units = gate_ref.shape
    count = grads_ref.shape[0]
    each = count // pieces
    rows = jnp.concatenate([ref[...] for ref in rows_refs], axis=0)
    both_ref[:count] = rows[:, :width]
    both_ref[count:] = rows[:, width : 2 * width]
    grads_ref[...] = rows[:, 2 * width :]
    rows_t_ref[...] = rows[:, width : 2 * width].T
    grads_t_ref[...] = rows[:, 2 * width :].T
    for i in range(units // chunk):
        at = slice(i * chunk, (i + 1) * chunk)
        gate_pre = dot_nn(both_ref[...], gate_ref[:, at])
        up_pre = dot_nn(both_ref[...], up_ref[:, at])
        sig = jax.nn.sigmoid(gate_pre)
        active = gate_pre * sig
        hidden = active * up_pre
        front_ref[:, at] = hidden[:count].astype(BF16)
        hidden_t_ref[at, :] = hidden[count:].T.astype(BF16)
        grad_hidden = dot_nn(down_ref[at, :], grads_t_ref[...]).T
        slope = up_pre[count:] * sig[count:] * (1.0 + gate_pre[count:] * (1.0 - sig[count:]))
        dgate = grad_hidden * slope
        dup = grad_hidden * active[count:]
        dgate_ref[:, at] = dgate.astype(BF16)
        dup_ref[:, at] = dup.astype(BF16)
        dgate_t_ref[at, :] = dgate.T.astype(BF16)
        dup_t_ref[at, :] = dup.T.astype(BF16)
    for j in range(width // tile):
        at = slice(j * tile, (j + 1) * tile)
        back = dot_nn(gate_ref[at, :], dgate_t_ref[...]) + dot_nn(up_ref[at, :], dup_t_ref[...])
        back = back.T.astype(BF16)
        front = dot_nn(front_ref[...], down_ref[:, at]).astype(BF16)
        for i, parts_ref in enumerate(parts_refs):
            own = slice(i * each, (i + 1) * each)
            parts_ref[:, at] = front[own]
            parts_ref[:, width + j * tile : width + (j + 1) * tile] = back[own]


def grads_kernel(
    wide,
    deep,
    rows_t_ref,
    hidden_t_ref,
    dgate_ref,
    dup_ref,
    grads_ref,
    mgate_ref,
    mup_ref,
    mdown_ref,
    ogate_ref,
    oup_ref,
    odown_ref,
):
    at = pl.ds(pl.multiple_of(pl.program_id(0) * wide, 16), wide)
    rows_t = rows_t_ref[at, :]
    ogate_ref[...] = (mgate_ref[at, :].astype(F32) + dot_nn(rows_t, dgate_ref[...])).astype(BF16)
    oup_ref[...] = (mup_ref[at, :].astype(F32) + dot_nn(rows_t, dup_ref[...])).astype(BF16)
    at = pl.ds(pl.multiple_of(pl.program_id(0) * deep, 16), deep)
    odown_ref[...] = (mdown_ref[at, :].astype(F32) + dot_nn(hidden_t_ref[at, :], grads_ref[...])).astype(BF16)


def combine_kernel(
    front_ref,
    upstream_ref,
    saved_ref,
    gain_ref,
    front_picks_ref,
    front_shares_ref,
    back_picks_ref,
    *refs,
):
    forward_ref, input_ref = refs[-2:]
    width = front_ref.shape[1]
    both = jnp.concatenate([ref[...] for ref in refs[:-2]], axis=0)
    parts = both[:, :width]
    forward_ref[...] = (
        front_ref[...].astype(F32)
        + front_shares_ref[0] * dot_nn(front_picks_ref[0], parts)
        + front_shares_ref[1] * dot_nn(front_picks_ref[1], parts)
    ).astype(BF16)
    gain = gain_ref[...].astype(F32)
    saved = saved_ref[...].astype(F32)
    inverse, _ = norm_rows(saved, gain)
    scaled = dot_nn(back_picks_ref[...], both[:, width:]) * gain
    cubed = inverse * inverse * inverse
    input_ref[...] = (
        upstream_ref[...].astype(F32)
        + inverse * scaled
        - cubed * saved * jnp.mean(scaled * saved, axis=-1, keepdims=True)
    ).astype(BF16)


def shape(dims, dtype=BF16):
    return jax.ShapeDtypeStruct(dims, dtype)


def held(dims, dtype=BF16):
    return pltpu.VMEM(dims, dtype)


def whole(memory_space=pltpu.VMEM):
    return pl.BlockSpec(memory_space=memory_space)


def cost(flops, moved):
    return pl.CostEstimate(flops=int(flops), bytes_accessed=int(moved), transcendentals=0)


def in_hbm(value):
    return pltpu.with_memory_space_constraint(value, pltpu.HBM)


def loaded(after, *arrays):
    amount = len(arrays)
    return pl.pallas_call(
        functools.partial(load_kernel, amount),
        out_shape=tuple(held(a.shape) for a in arrays),
        in_specs=[whole(pl.ANY)] * (1 + amount),
        out_specs=(whole(),) * amount,
        scratch_shapes=[pltpu.SemaphoreType.DMA((amount,))],
        compiler_params=pltpu.CompilerParams(vmem_limit_bytes=MIB),
        cost_estimate=cost(0, 2 * sum(a.size for a in arrays)),
        name="load_weights",
    )(after, *(in_hbm(a) for a in arrays))


def exchanged(pieces):
    if len(pieces) == 1:
        peers = lax.axis_size("ep")
        rows = pieces[0].reshape(peers, -1, pieces[0].shape[-1])
        return (lax.all_to_all(rows, "ep", split_axis=0, concat_axis=0, tiled=True).reshape(pieces[0].shape),)
    peers = range(len(pieces))
    return (pieces[0],) + tuple(lax.ppermute(pieces[i], "ep", [(j, j ^ i) for j in peers]) for i in peers[1:])


def ring(value, by):
    size = lax.axis_size("section")
    return lax.ppermute(value, "section", [(i, (i + by) % size) for i in range(size)])


def body(
    fresh_tokens,
    sent_forward,
    sent_backward,
    turn_gradient,
    saved_input,
    gain,
    ids_front,
    affinity_front,
    ids_back,
    affinity_back,
    w_gate,
    w_up,
    w_down,
    mirror_gate,
    mirror_up,
    mirror_down,
):
    peers = lax.axis_size("ep")
    groups = peers // EXPERTS
    tokens, width = fresh_tokens.shape
    capacity = max(groups, tokens * ids_front.shape[2] * 2 // EXPERTS)
    count = peers * capacity
    units = w_gate.shape[2]
    section_id = lax.axis_index("section")
    pieces = peers if peers <= 8 else 1
    flip = lax.axis_index("ep") if pieces > 1 else jnp.int32(0)
    place = jnp.stack([section_id, lax.axis_size("section") - 1 - section_id, flip]).astype(jnp.int32)
    returned = ring(sent_backward, -1)
    arrived = ring(sent_forward, 1)
    early = pl.pallas_call(
        functools.partial(early_kernel, capacity, groups),
        out_shape=(held((tokens, width)),) * 3
        + (
            held((1, width)),
            held((count, width)),
            held((count, tokens)),
            held((2, tokens, count)),
            held((2, tokens, 1), F32),
            held((count, tokens)),
            held((tokens, count)),
            held((count, 1), F32),
        ),
        in_specs=[whole(pltpu.SMEM)] + [whole(pl.ANY)] * 8,
        out_specs=(whole(),) * 11,
        scratch_shapes=[pltpu.VMEM((2, tokens), t) for t in (jnp.int32, F32, jnp.int32, F32)]
        + [pltpu.SemaphoreType.DMA((8,))],
        compiler_params=pltpu.CompilerParams(vmem_limit_bytes=4 * MIB),
        cost_estimate=cost(2 * count * tokens * width, 2 * count * width),
        name="early_rows",
    )(
        place,
        *(in_hbm(v) for v in (fresh_tokens, turn_gradient, saved_input[0], gain)),
        *(in_hbm(v[0].T) for v in (ids_front, affinity_front, ids_back, affinity_back)),
    )
    fresh, turn, saved, gain_row, back_rows = early[:5]
    front_table, front_picks, front_shares, back_table, back_picks, slot_shares = early[5:]
    front, upstream, *packed = pl.pallas_call(
        pack_kernel,
        out_shape=(held((tokens, width)),) * 2 + (shape((count // pieces, 3 * width)),) * pieces,
        in_specs=[whole(pltpu.SMEM)] + [whole()] * 9,
        out_specs=(whole(),) * (2 + pieces),
        compiler_params=pltpu.CompilerParams(vmem_limit_bytes=6 * MIB),
        cost_estimate=cost(2 * count * tokens * width * 4, 5 * count * width),
        name="pack_rows",
    )(
        place,
        arrived[0],
        fresh,
        returned[0],
        turn,
        gain_row,
        back_rows,
        front_table,
        back_table,
        slot_shares,
    )
    rows = exchanged(packed)
    (w_gate,) = loaded(packed[0], w_gate[0])
    chunk, tile = min(256, units), width // 7
    grads, rows_t, hidden_t, dgate, dup, *parts = pl.pallas_call(
        functools.partial(expert_kernel, chunk, tile, pieces),
        out_shape=(
            held((count, width)),
            held((width, count)),
            held((units, count)),
            held((count, units)),
            held((count, units)),
        )
        + (shape((count // pieces, 2 * width)),) * pieces,
        in_specs=[whole()] * (3 + pieces),
        out_specs=(whole(),) * (5 + pieces),
        scratch_shapes=[
            pltpu.VMEM((2 * count, width), BF16),
            pltpu.VMEM((width, count), BF16),
            pltpu.VMEM((units, count), BF16),
            pltpu.VMEM((units, count), BF16),
            pltpu.VMEM((count, units), BF16),
        ],
        compiler_params=pltpu.CompilerParams(vmem_limit_bytes=(6 if count <= 128 else 32) * MIB),
        cost_estimate=cost(2 * count * width * units * 8, 6 * width * units),
        name="expert_rows",
    )(w_gate, w_up[0], w_down[0], *rows)
    back = exchanged(parts)
    steps = 8
    wide, deep = width // steps, units // steps
    gate_spec = pl.BlockSpec((wide, units), lambda i: (i, 0))
    down_spec = pl.BlockSpec((deep, width), lambda i: (i, 0))
    out_gate, out_up, out_down = pl.pallas_call(
        functools.partial(grads_kernel, wide, deep),
        grid=(steps,),
        out_shape=(shape((width, units)), shape((width, units)), shape((units, width))),
        in_specs=[whole()] * 8,
        out_specs=(gate_spec, gate_spec, down_spec),
        compiler_params=pltpu.CompilerParams(vmem_limit_bytes=8 * MIB),
        cost_estimate=cost(2 * count * width * units * 3, 12 * width * units),
        name="weight_grads",
    )(rows_t, hidden_t, dgate, dup, grads, mirror_gate[0], mirror_up[0], mirror_down[0])
    forward_out, grad_input = pl.pallas_call(
        combine_kernel,
        out_shape=(shape((tokens, width)), shape((tokens, width))),
        in_specs=[whole()] * (7 + pieces),
        out_specs=(whole(),) * 2,
        compiler_params=pltpu.CompilerParams(vmem_limit_bytes=6 * MIB),
        cost_estimate=cost(2 * count * tokens * width * 3, 4 * count * width),
        name="combine_rows",
    )(front, upstream, saved, gain_row, front_picks, front_shares, back_picks, *back)
    return (forward_out[None], grad_input[None], out_gate[None], out_up[None], out_down[None])


def solution(mesh):
    return jax.shard_map(
        body,
        mesh=mesh,
        in_specs=(
            P("ep", None),
            P("section", "ep", None),
            P("section", "ep", None),
            P("ep", None),
            P("section", "ep", None),
            P("section", None),
            P("section", "ep", None),
            P("section", "ep", None),
            P("section", "ep", None),
            P("section", "ep", None),
            P("section", None, "ep"),
            P("section", None, "ep"),
            P("section", "ep", None),
            P("section", None, "ep"),
            P("section", None, "ep"),
            P("section", "ep", None),
        ),
        out_specs=(
            P("section", "ep", None),
            P("section", "ep", None),
            P("section", None, "ep"),
            P("section", None, "ep"),
            P("section", "ep", None),
        ),
        check_vma=False,
    )
```

```python
import functools

import jax
import jax.numpy as jnp
from jax import lax
from jax.experimental import pallas as pl
from jax.experimental.pallas import tpu as pltpu
from jax.sharding import PartitionSpec as P

EXPERTS = 8
F32 = jnp.float32
BF16 = jnp.bfloat16
MIB = 1 << 20


def dot_nn(a, b):
    return jnp.dot(a, b, preferred_element_type=F32)


def dot_nt(a, b):
    return lax.dot_general(a, b, (((1,), (1,)), ((), ())), preferred_element_type=F32)


def dot_tn(a, b):
    return lax.dot_general(a, b, (((0,), (0,)), ((), ())), preferred_element_type=F32)


def norm_rows(values, gain):
    inverse = lax.rsqrt(jnp.mean(values * values, axis=-1, keepdims=True) + 1e-06)
    return inverse, (values * inverse * gain).astype(BF16)


def choice_tables(ids, capacity, groups, flip):
    tokens = ids.shape[1]
    count = EXPERTS * groups * capacity
    row = lax.broadcasted_iota(jnp.int32, (count, tokens), 0)
    expert = ((row // capacity) ^ flip) // groups
    slot = (row % capacity).astype(F32)
    named = [(ids[j : j + 1, :] == expert).astype(F32) for j in range(2)]
    one = lax.broadcasted_iota(jnp.int32, (tokens, tokens), 0)
    other = lax.broadcasted_iota(jnp.int32, (tokens, tokens), 1)
    earlier = dot_nn((named[0] + named[1]).astype(BF16), (one < other).astype(BF16))
    here = (earlier == slot).astype(F32)
    return [n * here for n in named]


def shares_of(affinity):
    total = affinity[0:1, :] + affinity[1:2, :]
    return affinity[0:1, :] / total, affinity[1:2, :] / total


def as_column(row):
    size = row.shape[1]
    one = lax.broadcasted_iota(jnp.int32, (size, size), 0)
    other = lax.broadcasted_iota(jnp.int32, (size, size), 1)
    return jnp.sum(jnp.where(one == other, row, 0.0), axis=1, keepdims=True)


def early_kernel(
    capacity,
    groups,
    place_ref,
    forward_hbm,
    backward_hbm,
    fresh_hbm,
    turn_hbm,
    saved_hbm,
    gain_hbm,
    ids_front_hbm,
    aff_front_hbm,
    ids_back_hbm,
    aff_back_hbm,
    even_ref,
    odd_ref,
    fresh_ref,
    turn_ref,
    saved_ref,
    gain_ref,
    front_table_ref,
    front_picks_ref,
    front_shares_ref,
    back_table_ref,
    back_picks_ref,
    slot_shares_ref,
    *refs,
):
    rows_refs = refs[:-7]
    forward_ref, backward_ref, ids_front_ref, aff_front_ref, ids_back_ref, aff_back_ref, sems = refs[-7:]
    pairs = (
        (ids_front_hbm, ids_front_ref),
        (aff_front_hbm, aff_front_ref),
        (ids_back_hbm, ids_back_ref),
        (aff_back_hbm, aff_back_ref),
        (saved_hbm, saved_ref),
        (gain_hbm, gain_ref),
        (fresh_hbm, fresh_ref),
        (turn_hbm, turn_ref),
        (forward_hbm, forward_ref),
        (backward_hbm, backward_ref),
    )
    copies = [pltpu.make_async_copy(*pair, sems.at[i]) for i, pair in enumerate(pairs)]
    for copy in copies:
        copy.start()
    for copy in copies[:4]:
        copy.wait()
    flip = place_ref[2]
    first, second = choice_tables(ids_front_ref[...], capacity, groups, flip)
    front_table_ref[...] = (first + second).astype(BF16)
    front_picks_ref[0] = first.T.astype(BF16)
    front_picks_ref[1] = second.T.astype(BF16)
    share = shares_of(aff_front_ref[...])
    front_shares_ref[0] = as_column(share[0])
    front_shares_ref[1] = as_column(share[1])
    first, second = choice_tables(ids_back_ref[...], capacity, groups, flip)
    both = first + second
    back_table_ref[...] = both.astype(BF16)
    back_picks_ref[...] = both.T.astype(BF16)
    share = shares_of(aff_back_ref[...])
    slot_shares_ref[...] = jnp.sum(first * share[0] + second * share[1], axis=1, keepdims=True)
    copies[4].wait()
    copies[5].wait()
    _, normed = norm_rows(saved_ref[...].astype(F32), gain_ref[...].astype(F32))
    rows = dot_nn(back_table_ref[...], normed).astype(BF16)
    for i, rows_ref in enumerate(rows_refs):
        rows_ref[...] = rows[i * rows_ref.shape[0] : (i + 1) * rows_ref.shape[0]]
    for copy in copies[6:]:
        copy.wait()
    even = place_ref[3] == 0
    even_ref[...] = jnp.where(even, forward_ref[...].astype(F32), backward_ref[...].astype(F32)).astype(BF16)
    odd_ref[...] = jnp.where(even, backward_ref[...].astype(F32), forward_ref[...].astype(F32)).astype(BF16)


def pack_kernel(
    place_ref,
    even_ref,
    odd_ref,
    fresh_ref,
    turn_ref,
    gain_ref,
    front_table_ref,
    back_table_ref,
    slot_shares_ref,
    front_ref,
    upstream_ref,
    *packed_refs,
):
    width = fresh_ref.shape[1]
    even = place_ref[3] == 0
    by_even, by_odd = even_ref[...].astype(F32), odd_ref[...].astype(F32)
    front = jnp.where(place_ref[0] == 0, fresh_ref[...].astype(F32), jnp.where(even, by_odd, by_even))
    upstream = jnp.where(place_ref[1] == 0, turn_ref[...].astype(F32), jnp.where(even, by_even, by_odd))
    front_ref[...] = front.astype(BF16)
    upstream_ref[...] = upstream.astype(BF16)
    _, normed = norm_rows(front, gain_ref[...].astype(F32))
    front_rows = dot_nn(front_table_ref[...], normed).astype(BF16)
    grad_rows = (slot_shares_ref[...] * dot_nn(back_table_ref[...], upstream.astype(BF16))).astype(BF16)
    for i, packed_ref in enumerate(packed_refs):
        at = slice(i * packed_ref.shape[0], (i + 1) * packed_ref.shape[0])
        packed_ref[:, :width] = front_rows[at]
        packed_ref[:, width:] = grad_rows[at]


def split_kernel(pairs, after_hbm, *refs):
    del after_hbm
    keep_ref, give_ref = refs[pairs:]
    values = [ref[...] for ref in refs[:pairs]]
    half = values[0].shape[0] // 2
    keep_ref[...] = jnp.concatenate([value[:half] for value in values], axis=0)
    give_ref[...] = jnp.concatenate([value[half:] for value in values], axis=0)


def merge_kernel(keep_ref, arrived_ref, *pair_refs):
    keep, arrived = keep_ref[...], arrived_ref[...]
    each = keep.shape[0] // len(pair_refs)
    for i, pair_ref in enumerate(pair_refs):
        at = slice(i * each, (i + 1) * each)
        pair_ref[...] = jnp.concatenate([keep[at], arrived[at]], axis=0)


def load_kernel(amount, *refs):
    after, sources, targets, sems = refs[0], refs[1 : 1 + amount], refs[1 + amount : 1 + 2 * amount], refs[-1]
    del after
    copies = [pltpu.make_async_copy(a, b, sems.at[i]) for i, (a, b) in enumerate(zip(sources, targets))]
    for copy in copies:
        copy.start()
    for copy in copies:
        copy.wait()


def expert_kernel(
    chunk,
    tile,
    pieces,
    halves,
    gate_ref,
    up_ref,
    down_ref,
    *refs,
):
    rows_refs, back_refs, refs = refs[:pieces], refs[pieces : pieces + halves], refs[pieces + halves :]
    grads_ref, rows_t_ref, hidden_t_ref, dgate_ref, dup_ref = refs[:5]
    parts_refs = refs[5 : 5 + halves]
    both_ref, grads_t_ref, dgate_t_ref, dup_t_ref, front_ref = refs[5 + halves :]
    width, units = gate_ref.shape
    count = grads_ref.shape[0]
    each = count // halves
    order = [i for half in range(halves) for i in range(half, pieces, halves)]
    rows = jnp.concatenate([rows_refs[i][...] for i in order], axis=0)
    both_ref[:count] = rows[:, :width]
    grads_ref[...] = rows[:, width:]
    grads_t_ref[...] = rows[:, width:].T
    rows = jnp.concatenate([ref[...] for ref in back_refs], axis=0)
    both_ref[count:] = rows
    rows_t_ref[...] = rows.T
    for i in range(units // chunk):
        at = slice(i * chunk, (i + 1) * chunk)
        gate_pre = dot_nn(both_ref[...], gate_ref[:, at])
        up_pre = dot_nn(both_ref[...], up_ref[:, at])
        sig = jax.nn.sigmoid(gate_pre)
        active = gate_pre * sig
        hidden = active * up_pre
        front_ref[:, at] = hidden[:count].astype(BF16)
        hidden_t_ref[at, :] = hidden[count:].T.astype(BF16)
        grad_hidden = dot_nn(down_ref[at, :], grads_t_ref[...]).T
        slope = up_pre[count:] * sig[count:] * (1.0 + gate_pre[count:] * (1.0 - sig[count:]))
        dgate = grad_hidden * slope
        dup = grad_hidden * active[count:]
        dgate_ref[:, at] = dgate.astype(BF16)
        dup_ref[:, at] = dup.astype(BF16)
        dgate_t_ref[at, :] = dgate.T.astype(BF16)
        dup_t_ref[at, :] = dup.T.astype(BF16)
    for j in range(width // tile):
        at = slice(j * tile, (j + 1) * tile)
        back = dot_nn(gate_ref[at, :], dgate_t_ref[...]) + dot_nn(up_ref[at, :], dup_t_ref[...])
        back = back.T.astype(BF16)
        front = dot_nn(front_ref[...], down_ref[:, at]).astype(BF16)
        for i, parts_ref in enumerate(parts_refs):
            own = slice(i * each, (i + 1) * each)
            parts_ref[:, at] = front[own]
            parts_ref[:, width + j * tile : width + (j + 1) * tile] = back[own]


def grads_kernel(slots, tile, by_rows, after_hbm, *refs):
    del after_hbm
    amount = len(by_rows)
    mirrors, lefts, rights, outs = (refs[i * amount : (i + 1) * amount] for i in range(4))
    bufs, sems = refs[4 * amount : 5 * amount], refs[-1]
    steps = [out.shape[0 if rows else 1] // tile for out, rows in zip(outs, by_rows)]

    def copy(i, j):
        at = pl.ds(i * tile, tile)
        target = outs[j].at[at, :] if by_rows[j] else outs[j].at[:, at]
        return pltpu.make_async_copy(bufs[j].at[i % slots], target, sems.at[j, i % slots])

    for i in range(max(steps)):
        for j in range(amount):
            if i >= slots:
                copy(i - slots, j).wait()
            at = slice(i * tile, (i + 1) * tile)
            if by_rows[j]:
                total = mirrors[j][at, :].astype(F32) + dot_nn(lefts[j][at, :], rights[j][...])
            else:
                total = mirrors[j][:, at].astype(F32) + dot_nn(lefts[j][...], rights[j][:, at])
            bufs[j][i % slots] = total.astype(BF16)
            copy(i, j).start()
    for j in range(amount):
        for i in range(max(steps[j] - slots, 0), steps[j]):
            copy(i, j).wait()


def combine_kernel(
    front_ref,
    upstream_ref,
    saved_ref,
    gain_ref,
    front_picks_ref,
    front_shares_ref,
    back_picks_ref,
    *refs,
):
    forward_ref, input_ref = refs[-2:]
    width = front_ref.shape[1]
    both = jnp.concatenate([ref[...] for ref in refs[:-2]], axis=0)
    parts = both[:, :width]
    forward_ref[...] = (
        front_ref[...].astype(F32)
        + front_shares_ref[0] * dot_nn(front_picks_ref[0], parts)
        + front_shares_ref[1] * dot_nn(front_picks_ref[1], parts)
    ).astype(BF16)
    gain = gain_ref[...].astype(F32)
    saved = saved_ref[...].astype(F32)
    inverse, _ = norm_rows(saved, gain)
    scaled = dot_nn(back_picks_ref[...], both[:, width:]) * gain
    cubed = inverse * inverse * inverse
    input_ref[...] = (
        upstream_ref[...].astype(F32)
        + inverse * scaled
        - cubed * saved * jnp.mean(scaled * saved, axis=-1, keepdims=True)
    ).astype(BF16)


def shape(dims, dtype=BF16):
    return jax.ShapeDtypeStruct(dims, dtype)


def held(dims, dtype=BF16):
    return pltpu.VMEM(dims, dtype)


def whole(memory_space=pltpu.VMEM):
    return pl.BlockSpec(memory_space=memory_space)


def cost(flops, moved):
    return pl.CostEstimate(flops=int(flops), bytes_accessed=int(moved), transcendentals=0)


def in_hbm(value):
    return pltpu.with_memory_space_constraint(value, pltpu.HBM)


def loaded(after, *arrays):
    amount = len(arrays)
    return pl.pallas_call(
        functools.partial(load_kernel, amount),
        out_shape=tuple(held(a.shape) for a in arrays),
        in_specs=[whole(pl.ANY)] * (1 + amount),
        out_specs=(whole(),) * amount,
        scratch_shapes=[pltpu.SemaphoreType.DMA((amount,))],
        compiler_params=pltpu.CompilerParams(vmem_limit_bytes=MIB),
        cost_estimate=cost(0, 2 * sum(a.size for a in arrays)),
        name="load_weights",
    )(after, *(in_hbm(a) for a in arrays))


def exchanged(pieces, step=1):
    if len(pieces) == 1:
        peers = lax.axis_size("ep")
        rows = pieces[0].reshape(peers, -1, pieces[0].shape[-1])
        return (lax.all_to_all(rows, "ep", split_axis=0, concat_axis=0, tiled=True).reshape(pieces[0].shape),)
    peers = range(lax.axis_size("ep"))
    order = range(len(pieces) - 1, 0, -1)
    sent = {i: lax.ppermute(pieces[i], "ep", [(j, j ^ (i * step)) for j in peers]) for i in order}
    return (pieces[0], *(sent[i] for i in range(1, len(pieces))))


def swapped(halves):
    if len(halves) == 1:
        return halves
    peers = range(lax.axis_size("ep"))
    return halves[0], lax.ppermute(halves[1], "ep", [(j, j ^ 1) for j in peers])


def split(pairs, after):
    if len(pairs) == 1:
        return pairs
    count, width = pairs[0].shape
    count = count * len(pairs) // 2
    keep, give = pl.pallas_call(
        functools.partial(split_kernel, len(pairs)),
        out_shape=(shape((count, width)),) * 2,
        in_specs=[whole(pl.ANY)] + [whole()] * len(pairs),
        out_specs=(whole(),) * 2,
        compiler_params=pltpu.CompilerParams(vmem_limit_bytes=4 * MIB),
        cost_estimate=cost(0, 8 * count * width),
        name="split_rows",
    )(after, *pairs)
    return swapped((keep, give))


def merged(halves):
    if len(halves) == 1:
        return halves
    count, width = halves[0].shape
    return pl.pallas_call(
        merge_kernel,
        out_shape=(shape((count // 2, width)),) * 4,
        in_specs=[whole()] * 2,
        out_specs=(whole(),) * 4,
        compiler_params=pltpu.CompilerParams(vmem_limit_bytes=4 * MIB),
        cost_estimate=cost(0, 8 * count * width),
        name="merge_rows",
    )(*halves)


def weight_grads(after, mirrors, lefts, rights, by_rows):
    slots, tile = 4 // len(mirrors) + 1, 512
    tiles = [(tile, m.shape[1]) if rows else (m.shape[0], tile) for m, rows in zip(mirrors, by_rows)]
    size = sum(m.size for m in mirrors)
    return pl.pallas_call(
        functools.partial(grads_kernel, slots, tile, by_rows),
        out_shape=tuple(shape(m.shape) for m in mirrors),
        in_specs=[whole(pl.ANY)] + [whole()] * (3 * len(mirrors)),
        out_specs=(whole(pl.ANY),) * len(mirrors),
        scratch_shapes=[pltpu.VMEM((slots, *t), BF16) for t in tiles]
        + [pltpu.SemaphoreType.DMA((len(mirrors), slots))],
        compiler_params=pltpu.CompilerParams(vmem_limit_bytes=10 * MIB),
        cost_estimate=cost(2 * size * rights[0].shape[0], 4 * size),
        name="weight_grads",
    )(after, *mirrors, *lefts, *rights)


def beside(value, first):
    size = lax.axis_size("section")
    pairs = [(i, i + 1 if (i - first) % 2 == 0 else i - 1) for i in range(size)]
    return lax.ppermute(value, "section", [(i, j if 0 <= j < size else i) for i, j in pairs])


def body(
    fresh_tokens,
    sent_forward,
    sent_backward,
    turn_gradient,
    saved_input,
    gain,
    ids_front,
    affinity_front,
    ids_back,
    affinity_back,
    w_gate,
    w_up,
    w_down,
    mirror_gate,
    mirror_up,
    mirror_down,
):
    peers = lax.axis_size("ep")
    groups = peers // EXPERTS
    tokens, width = fresh_tokens.shape
    capacity = max(groups, tokens * ids_front.shape[2] * 2 // EXPERTS)
    count = peers * capacity
    units = w_gate.shape[2]
    section_id = lax.axis_index("section")
    pieces, pairs, halves = (8, 4, 2) if peers == 8 else (1, 1, 1)
    flip = lax.axis_index("ep") if pieces > 1 else jnp.int32(0)
    place = jnp.stack([section_id, lax.axis_size("section") - 1 - section_id, flip, section_id % 2]).astype(jnp.int32)
    early = pl.pallas_call(
        functools.partial(early_kernel, capacity, groups),
        out_shape=(shape((tokens, width)),) * 2
        + (held((tokens, width)),) * 3
        + (
            held((1, width)),
            held((count, tokens)),
            held((2, tokens, count)),
            held((2, tokens, 1), F32),
            held((count, tokens)),
            held((tokens, count)),
            held((count, 1), F32),
        )
        + (shape((count // pairs, width)),) * pairs,
        in_specs=[whole(pltpu.SMEM)] + [whole(pl.ANY)] * 10,
        out_specs=(whole(),) * (12 + pairs),
        scratch_shapes=[pltpu.VMEM((tokens, width), BF16)] * 2
        + [pltpu.VMEM((2, tokens), t) for t in (jnp.int32, F32, jnp.int32, F32)]
        + [pltpu.SemaphoreType.DMA((10,))],
        compiler_params=pltpu.CompilerParams(vmem_limit_bytes=4 * MIB),
        cost_estimate=cost(2 * count * tokens * width, 2 * count * width),
        name="early_rows",
    )(
        place,
        *(in_hbm(v) for v in (sent_forward[0], sent_backward[0], fresh_tokens, turn_gradient, saved_input[0], gain)),
        *(in_hbm(v[0].T) for v in (ids_front, affinity_front, ids_back, affinity_back)),
    )
    by_even, by_odd = (beside(early[i], i) for i in range(2))
    fresh, turn, saved, gain_row = early[2:6]
    front_table, front_picks, front_shares, back_table, back_picks, slot_shares = early[6:12]
    back_pairs = exchanged(early[12:], 2)
    front, upstream, *packed = pl.pallas_call(
        pack_kernel,
        out_shape=(held((tokens, width)),) * 2 + (shape((count // pieces, 2 * width)),) * pieces,
        in_specs=[whole(pltpu.SMEM)] + [whole()] * 8,
        out_specs=(whole(),) * (2 + pieces),
        compiler_params=pltpu.CompilerParams(vmem_limit_bytes=6 * MIB),
        cost_estimate=cost(2 * count * tokens * width * 4, 5 * count * width),
        name="pack_rows",
    )(
        place,
        by_even,
        by_odd,
        fresh,
        turn,
        gain_row,
        front_table,
        back_table,
        slot_shares,
    )
    rows = exchanged(packed)
    (w_gate,) = loaded(rows[len(rows) * 3 // 8], w_gate[0])
    back_rows = split(back_pairs, packed[0])
    chunk, tile = min(256, units), width // 7
    grads, rows_t, hidden_t, dgate, dup, *parts = pl.pallas_call(
        functools.partial(expert_kernel, chunk, tile, pieces, halves),
        out_shape=(
            held((count, width)),
            held((width, count)),
            held((units, count)),
            held((count, units)),
            held((count, units)),
        )
        + (shape((count // halves, 2 * width)),) * halves,
        in_specs=[whole()] * (3 + pieces + halves),
        out_specs=(whole(),) * (5 + halves),
        scratch_shapes=[
            pltpu.VMEM((2 * count, width), BF16),
            pltpu.VMEM((width, count), BF16),
            pltpu.VMEM((units, count), BF16),
            pltpu.VMEM((units, count), BF16),
            pltpu.VMEM((count, units), BF16),
        ],
        compiler_params=pltpu.CompilerParams(vmem_limit_bytes=(6 if count <= 128 else 32) * MIB),
        cost_estimate=cost(2 * count * width * units * 8, 6 * width * units),
        name="expert_rows",
    )(w_gate, w_up[0], w_down[0], *rows, *back_rows)
    neighbour = swapped(parts)
    (out_gate,) = weight_grads(parts[0], (mirror_gate[0],), (rows_t,), (dgate,), (True,))
    back = exchanged(merged(neighbour), 2)
    out_up, out_down = weight_grads(
        back[0], (mirror_up[0], mirror_down[0]), (rows_t, hidden_t), (dup, grads), (True, False)
    )
    forward_out, grad_input = pl.pallas_call(
        combine_kernel,
        out_shape=(shape((tokens, width)), shape((tokens, width))),
        in_specs=[whole()] * (7 + pairs),
        out_specs=(whole(),) * 2,
        compiler_params=pltpu.CompilerParams(vmem_limit_bytes=6 * MIB),
        cost_estimate=cost(2 * count * tokens * width * 3, 4 * count * width),
        name="combine_rows",
    )(front, upstream, saved, gain_row, front_picks, front_shares, back_picks, *back)
    return (forward_out[None], grad_input[None], out_gate[None], out_up[None], out_down[None])


def solution(mesh):
    return jax.shard_map(
        body,
        mesh=mesh,
        in_specs=(
            P("ep", None),
            P("section", "ep", None),
            P("section", "ep", None),
            P("ep", None),
            P("section", "ep", None),
            P("section", None),
            P("section", "ep", None),
            P("section", "ep", None),
            P("section", "ep", None),
            P("section", "ep", None),
            P("section", None, "ep"),
            P("section", None, "ep"),
            P("section", "ep", None),
            P("section", None, "ep"),
            P("section", None, "ep"),
            P("section", "ep", None),
        ),
        out_specs=(
            P("section", "ep", None),
            P("section", "ep", None),
            P("section", None, "ep"),
            P("section", None, "ep"),
            P("section", "ep", None),
        ),
        check_vma=False,
    )
```

```python
import functools

import jax
import jax.numpy as jnp
from jax import lax
from jax.experimental import pallas as pl
from jax.experimental.pallas import tpu as pltpu
from jax.sharding import PartitionSpec as P

EXPERTS = 8
F32 = jnp.float32
BF16 = jnp.bfloat16
MIB = 1 << 20


def dot_nn(a, b):
    return jnp.dot(a, b, preferred_element_type=F32)


def dot_nt(a, b):
    return lax.dot_general(a, b, (((1,), (1,)), ((), ())), preferred_element_type=F32)


def dot_tn(a, b):
    return lax.dot_general(a, b, (((0,), (0,)), ((), ())), preferred_element_type=F32)


def norm_rows(values, gain):
    inverse = lax.rsqrt(jnp.mean(values * values, axis=-1, keepdims=True) + 1e-06)
    return inverse, (values * inverse * gain).astype(BF16)


def choice_tables(ids, capacity, groups, flip):
    tokens = ids.shape[1]
    count = EXPERTS * groups * capacity
    row = lax.broadcasted_iota(jnp.int32, (count, tokens), 0)
    expert = ((row // capacity) ^ flip) // groups
    slot = (row % capacity).astype(F32)
    named = [(ids[j : j + 1, :] == expert).astype(F32) for j in range(2)]
    one = lax.broadcasted_iota(jnp.int32, (tokens, tokens), 0)
    other = lax.broadcasted_iota(jnp.int32, (tokens, tokens), 1)
    earlier = dot_nn((named[0] + named[1]).astype(BF16), (one < other).astype(BF16))
    here = (earlier == slot).astype(F32)
    return [n * here for n in named]


def shares_of(affinity):
    total = affinity[0:1, :] + affinity[1:2, :]
    return affinity[0:1, :] / total, affinity[1:2, :] / total


def as_column(row):
    size = row.shape[1]
    one = lax.broadcasted_iota(jnp.int32, (size, size), 0)
    other = lax.broadcasted_iota(jnp.int32, (size, size), 1)
    return jnp.sum(jnp.where(one == other, row, 0.0), axis=1, keepdims=True)


def early_kernel(
    capacity,
    groups,
    place_ref,
    forward_hbm,
    backward_hbm,
    fresh_hbm,
    turn_hbm,
    saved_hbm,
    gain_hbm,
    ids_front_hbm,
    aff_front_hbm,
    ids_back_hbm,
    aff_back_hbm,
    even_ref,
    odd_ref,
    fresh_ref,
    turn_ref,
    saved_ref,
    gain_ref,
    front_table_ref,
    front_picks_ref,
    front_shares_ref,
    back_table_ref,
    back_picks_ref,
    slot_shares_ref,
    *refs,
):
    rows_refs = refs[:-7]
    forward_ref, backward_ref, ids_front_ref, aff_front_ref, ids_back_ref, aff_back_ref, sems = refs[-7:]
    pairs = (
        (ids_front_hbm, ids_front_ref),
        (aff_front_hbm, aff_front_ref),
        (ids_back_hbm, ids_back_ref),
        (aff_back_hbm, aff_back_ref),
        (saved_hbm, saved_ref),
        (gain_hbm, gain_ref),
        (fresh_hbm, fresh_ref),
        (turn_hbm, turn_ref),
        (forward_hbm, forward_ref),
        (backward_hbm, backward_ref),
    )
    copies = [pltpu.make_async_copy(*pair, sems.at[i]) for i, pair in enumerate(pairs)]
    for copy in copies:
        copy.start()
    for copy in copies[:4]:
        copy.wait()
    flip = place_ref[2]
    first, second = choice_tables(ids_front_ref[...], capacity, groups, flip)
    front_table_ref[...] = (first + second).astype(BF16)
    front_picks_ref[0] = first.T.astype(BF16)
    front_picks_ref[1] = second.T.astype(BF16)
    share = shares_of(aff_front_ref[...])
    front_shares_ref[0] = as_column(share[0])
    front_shares_ref[1] = as_column(share[1])
    first, second = choice_tables(ids_back_ref[...], capacity, groups, flip)
    both = first + second
    back_table_ref[...] = both.astype(BF16)
    back_picks_ref[...] = both.T.astype(BF16)
    share = shares_of(aff_back_ref[...])
    slot_shares_ref[...] = jnp.sum(first * share[0] + second * share[1], axis=1, keepdims=True)
    copies[4].wait()
    copies[5].wait()
    _, normed = norm_rows(saved_ref[...].astype(F32), gain_ref[...].astype(F32))
    rows = dot_nn(back_table_ref[...], normed).astype(BF16)
    for i, rows_ref in enumerate(rows_refs):
        rows_ref[...] = rows[i * rows_ref.shape[0] : (i + 1) * rows_ref.shape[0]]
    for copy in copies[6:]:
        copy.wait()
    even = place_ref[3] == 0
    even_ref[...] = jnp.where(even, forward_ref[...].astype(F32), backward_ref[...].astype(F32)).astype(BF16)
    odd_ref[...] = jnp.where(even, backward_ref[...].astype(F32), forward_ref[...].astype(F32)).astype(BF16)


def pack_kernel(
    place_ref,
    even_ref,
    odd_ref,
    fresh_ref,
    turn_ref,
    gain_ref,
    front_table_ref,
    back_table_ref,
    slot_shares_ref,
    front_ref,
    upstream_ref,
    *packed_refs,
):
    width = fresh_ref.shape[1]
    even = place_ref[3] == 0
    by_even, by_odd = even_ref[...].astype(F32), odd_ref[...].astype(F32)
    front = jnp.where(place_ref[0] == 0, fresh_ref[...].astype(F32), jnp.where(even, by_odd, by_even))
    upstream = jnp.where(place_ref[1] == 0, turn_ref[...].astype(F32), jnp.where(even, by_even, by_odd))
    front_ref[...] = front.astype(BF16)
    upstream_ref[...] = upstream.astype(BF16)
    _, normed = norm_rows(front, gain_ref[...].astype(F32))
    front_rows = dot_nn(front_table_ref[...], normed).astype(BF16)
    grad_rows = (slot_shares_ref[...] * dot_nn(back_table_ref[...], upstream.astype(BF16))).astype(BF16)
    for i, packed_ref in enumerate(packed_refs):
        at = slice(i * packed_ref.shape[0], (i + 1) * packed_ref.shape[0])
        packed_ref[:, :width] = front_rows[at]
        packed_ref[:, width:] = grad_rows[at]


def split_kernel(pairs, after_hbm, *refs):
    del after_hbm
    keep_ref, give_ref = refs[pairs:]
    values = [ref[...] for ref in refs[:pairs]]
    half = values[0].shape[0] // 2
    keep_ref[...] = jnp.concatenate([value[:half] for value in values], axis=0)
    give_ref[...] = jnp.concatenate([value[half:] for value in values], axis=0)


def merge_kernel(keep_ref, arrived_ref, *pair_refs):
    keep, arrived = keep_ref[...], arrived_ref[...]
    each = keep.shape[0] // len(pair_refs)
    for i, pair_ref in enumerate(pair_refs):
        at = slice(i * each, (i + 1) * each)
        pair_ref[...] = jnp.concatenate([keep[at], arrived[at]], axis=0)


def load_kernel(amount, *refs):
    after, sources, targets, sems = refs[0], refs[1 : 1 + amount], refs[1 + amount : 1 + 2 * amount], refs[-1]
    del after
    copies = [pltpu.make_async_copy(a, b, sems.at[i]) for i, (a, b) in enumerate(zip(sources, targets))]
    for copy in copies:
        copy.start()
    for copy in copies:
        copy.wait()


def expert_kernel(
    chunk,
    tile,
    pieces,
    halves,
    gate_ref,
    up_ref,
    down_ref,
    *refs,
):
    rows_refs, back_refs, refs = refs[:pieces], refs[pieces : pieces + halves], refs[pieces + halves :]
    grads_ref, rows_t_ref, hidden_t_ref, dgate_ref, dup_ref = refs[:5]
    parts_refs = refs[5 : 5 + halves]
    both_ref, grads_t_ref, dgate_t_ref, dup_t_ref, front_ref = refs[5 + halves :]
    width, units = gate_ref.shape
    count = grads_ref.shape[0]
    each = count // halves
    order = [i for half in range(halves) for i in range(half, pieces, halves)]
    rows = jnp.concatenate([rows_refs[i][...] for i in order], axis=0)
    both_ref[:count] = rows[:, :width]
    grads_ref[...] = rows[:, width:]
    grads_t_ref[...] = rows[:, width:].T
    rows = jnp.concatenate([ref[...] for ref in back_refs], axis=0)
    both_ref[count:] = rows
    rows_t_ref[...] = rows.T
    for i in range(units // chunk):
        at = slice(i * chunk, (i + 1) * chunk)
        gate_pre = dot_nn(both_ref[...], gate_ref[:, at])
        up_pre = dot_nn(both_ref[...], up_ref[:, at])
        sig = jax.nn.sigmoid(gate_pre)
        active = gate_pre * sig
        hidden = active * up_pre
        front_ref[:, at] = hidden[:count].astype(BF16)
        hidden_t_ref[at, :] = hidden[count:].T.astype(BF16)
        grad_hidden = dot_nn(down_ref[at, :], grads_t_ref[...]).T
        slope = up_pre[count:] * sig[count:] * (1.0 + gate_pre[count:] * (1.0 - sig[count:]))
        dgate = grad_hidden * slope
        dup = grad_hidden * active[count:]
        dgate_ref[:, at] = dgate.astype(BF16)
        dup_ref[:, at] = dup.astype(BF16)
        dgate_t_ref[at, :] = dgate.T.astype(BF16)
        dup_t_ref[at, :] = dup.T.astype(BF16)
    for j in range(width // tile):
        at = slice(j * tile, (j + 1) * tile)
        back = dot_nn(gate_ref[at, :], dgate_t_ref[...]) + dot_nn(up_ref[at, :], dup_t_ref[...])
        back = back.T.astype(BF16)
        front = dot_nn(front_ref[...], down_ref[:, at]).astype(BF16)
        for i, parts_ref in enumerate(parts_refs):
            own = slice(i * each, (i + 1) * each)
            parts_ref[:, at] = front[own]
            parts_ref[:, width + j * tile : width + (j + 1) * tile] = back[own]


def grads_kernel(slots, tile, by_rows, after_hbm, *refs):
    del after_hbm
    amount = len(by_rows)
    mirrors, lefts, rights, outs = (refs[i * amount : (i + 1) * amount] for i in range(4))
    bufs, sems = refs[4 * amount : 5 * amount], refs[-1]
    steps = [out.shape[0 if rows else 1] // tile for out, rows in zip(outs, by_rows)]

    def copy(i, j):
        at = pl.ds(i * tile, tile)
        target = outs[j].at[at, :] if by_rows[j] else outs[j].at[:, at]
        return pltpu.make_async_copy(bufs[j].at[i % slots], target, sems.at[j, i % slots])

    for i in range(max(steps)):
        for j in range(amount):
            if i >= slots:
                copy(i - slots, j).wait()
            at = slice(i * tile, (i + 1) * tile)
            if by_rows[j]:
                total = mirrors[j][at, :].astype(F32) + dot_nn(lefts[j][at, :], rights[j][...])
            else:
                total = mirrors[j][:, at].astype(F32) + dot_nn(lefts[j][...], rights[j][:, at])
            bufs[j][i % slots] = total.astype(BF16)
            copy(i, j).start()
    for j in range(amount):
        for i in range(max(steps[j] - slots, 0), steps[j]):
            copy(i, j).wait()


def combine_kernel(
    front_ref,
    upstream_ref,
    saved_ref,
    gain_ref,
    front_picks_ref,
    front_shares_ref,
    back_picks_ref,
    *refs,
):
    forward_ref, input_ref = refs[-2:]
    width = front_ref.shape[1]
    both = jnp.concatenate([refs[i][...] for i in ((0, 2, 3, 1) if len(refs) == 6 else (0,))], axis=0)
    parts = both[:, :width]
    forward_ref[...] = (
        front_ref[...].astype(F32)
        + front_shares_ref[0] * dot_nn(front_picks_ref[0], parts)
        + front_shares_ref[1] * dot_nn(front_picks_ref[1], parts)
    ).astype(BF16)
    gain = gain_ref[...].astype(F32)
    saved = saved_ref[...].astype(F32)
    inverse, _ = norm_rows(saved, gain)
    scaled = dot_nn(back_picks_ref[...], both[:, width:]) * gain
    cubed = inverse * inverse * inverse
    input_ref[...] = (
        upstream_ref[...].astype(F32)
        + inverse * scaled
        - cubed * saved * jnp.mean(scaled * saved, axis=-1, keepdims=True)
    ).astype(BF16)


def shape(dims, dtype=BF16):
    return jax.ShapeDtypeStruct(dims, dtype)


def held(dims, dtype=BF16):
    return pltpu.VMEM(dims, dtype)


def whole(memory_space=pltpu.VMEM):
    return pl.BlockSpec(memory_space=memory_space)


def cost(flops, moved):
    return pl.CostEstimate(flops=int(flops), bytes_accessed=int(moved), transcendentals=0)


def in_hbm(value):
    return pltpu.with_memory_space_constraint(value, pltpu.HBM)


def loaded(after, *arrays):
    amount = len(arrays)
    return pl.pallas_call(
        functools.partial(load_kernel, amount),
        out_shape=tuple(held(a.shape) for a in arrays),
        in_specs=[whole(pl.ANY)] * (1 + amount),
        out_specs=(whole(),) * amount,
        scratch_shapes=[pltpu.SemaphoreType.DMA((amount,))],
        compiler_params=pltpu.CompilerParams(vmem_limit_bytes=MIB),
        cost_estimate=cost(0, 2 * sum(a.size for a in arrays)),
        name="load_weights",
    )(after, *(in_hbm(a) for a in arrays))


def exchanged(pieces, step=1):
    if len(pieces) == 1:
        peers = lax.axis_size("ep")
        rows = pieces[0].reshape(peers, -1, pieces[0].shape[-1])
        return (lax.all_to_all(rows, "ep", split_axis=0, concat_axis=0, tiled=True).reshape(pieces[0].shape),)
    peers = range(lax.axis_size("ep"))
    order = range(len(pieces) - 1, 0, -1)
    sent = {i: lax.ppermute(pieces[i], "ep", [(j, j ^ (i * step)) for j in peers]) for i in order}
    return (pieces[0], *(sent[i] for i in range(1, len(pieces))))


def swapped(halves):
    if len(halves) == 1:
        return halves
    peers = range(lax.axis_size("ep"))
    return halves[0], lax.ppermute(halves[1], "ep", [(j, j ^ 1) for j in peers])


def split(pairs, after):
    if len(pairs) == 1:
        return pairs
    count, width = pairs[0].shape
    count = count * len(pairs) // 2
    keep, give = pl.pallas_call(
        functools.partial(split_kernel, len(pairs)),
        out_shape=(shape((count, width)),) * 2,
        in_specs=[whole(pl.ANY)] + [whole()] * len(pairs),
        out_specs=(whole(),) * 2,
        compiler_params=pltpu.CompilerParams(vmem_limit_bytes=4 * MIB),
        cost_estimate=cost(0, 8 * count * width),
        name="split_rows",
    )(after, *pairs)
    return swapped((keep, give))


def merged(halves):
    if len(halves) == 1:
        return halves
    count, width = halves[0].shape
    return pl.pallas_call(
        merge_kernel,
        out_shape=(shape((count // 2, width)),) * 4,
        in_specs=[whole()] * 2,
        out_specs=(whole(),) * 4,
        compiler_params=pltpu.CompilerParams(vmem_limit_bytes=4 * MIB),
        cost_estimate=cost(0, 8 * count * width),
        name="merge_rows",
    )(*halves)


def weight_grads(after, mirrors, lefts, rights, by_rows):
    slots, tile = 4 // len(mirrors) + 1, 512
    tiles = [(tile, m.shape[1]) if rows else (m.shape[0], tile) for m, rows in zip(mirrors, by_rows)]
    size = sum(m.size for m in mirrors)
    return pl.pallas_call(
        functools.partial(grads_kernel, slots, tile, by_rows),
        out_shape=tuple(shape(m.shape) for m in mirrors),
        in_specs=[whole(pl.ANY)] + [whole()] * (3 * len(mirrors)),
        out_specs=(whole(pl.ANY),) * len(mirrors),
        scratch_shapes=[pltpu.VMEM((slots, *t), BF16) for t in tiles]
        + [pltpu.SemaphoreType.DMA((len(mirrors), slots))],
        compiler_params=pltpu.CompilerParams(vmem_limit_bytes=10 * MIB),
        cost_estimate=cost(2 * size * rights[0].shape[0], 4 * size),
        name="weight_grads",
    )(after, *mirrors, *lefts, *rights)


def beside(value, first):
    size = lax.axis_size("section")
    pairs = [(i, i + 1 if (i - first) % 2 == 0 else i - 1) for i in range(size)]
    return lax.ppermute(value, "section", [(i, j if 0 <= j < size else i) for i, j in pairs])


def body(
    fresh_tokens,
    sent_forward,
    sent_backward,
    turn_gradient,
    saved_input,
    gain,
    ids_front,
    affinity_front,
    ids_back,
    affinity_back,
    w_gate,
    w_up,
    w_down,
    mirror_gate,
    mirror_up,
    mirror_down,
):
    peers = lax.axis_size("ep")
    groups = peers // EXPERTS
    tokens, width = fresh_tokens.shape
    capacity = max(groups, tokens * ids_front.shape[2] * 2 // EXPERTS)
    count = peers * capacity
    units = w_gate.shape[2]
    section_id = lax.axis_index("section")
    pieces, pairs, halves = (8, 4, 2) if peers == 8 else (1, 1, 1)
    flip = lax.axis_index("ep") if pieces > 1 else jnp.int32(0)
    place = jnp.stack([section_id, lax.axis_size("section") - 1 - section_id, flip, section_id % 2]).astype(jnp.int32)
    early = pl.pallas_call(
        functools.partial(early_kernel, capacity, groups),
        out_shape=(shape((tokens, width)),) * 2
        + (held((tokens, width)),) * 3
        + (
            held((1, width)),
            held((count, tokens)),
            held((2, tokens, count)),
            held((2, tokens, 1), F32),
            held((count, tokens)),
            held((tokens, count)),
            held((count, 1), F32),
        )
        + (shape((count // pairs, width)),) * pairs,
        in_specs=[whole(pltpu.SMEM)] + [whole(pl.ANY)] * 10,
        out_specs=(whole(),) * (12 + pairs),
        scratch_shapes=[pltpu.VMEM((tokens, width), BF16)] * 2
        + [pltpu.VMEM((2, tokens), t) for t in (jnp.int32, F32, jnp.int32, F32)]
        + [pltpu.SemaphoreType.DMA((10,))],
        compiler_params=pltpu.CompilerParams(vmem_limit_bytes=4 * MIB),
        cost_estimate=cost(2 * count * tokens * width, 2 * count * width),
        name="early_rows",
    )(
        place,
        *(in_hbm(v) for v in (sent_forward[0], sent_backward[0], fresh_tokens, turn_gradient, saved_input[0], gain)),
        *(in_hbm(v[0].T) for v in (ids_front, affinity_front, ids_back, affinity_back)),
    )
    by_even, by_odd = (beside(early[i], i) for i in range(2))
    fresh, turn, saved, gain_row = early[2:6]
    front_table, front_picks, front_shares, back_table, back_picks, slot_shares = early[6:12]
    back_pairs = exchanged(early[12:], 2)
    front, upstream, *packed = pl.pallas_call(
        pack_kernel,
        out_shape=(held((tokens, width)),) * 2 + (shape((count // pieces, 2 * width)),) * pieces,
        in_specs=[whole(pltpu.SMEM)] + [whole()] * 8,
        out_specs=(whole(),) * (2 + pieces),
        compiler_params=pltpu.CompilerParams(vmem_limit_bytes=6 * MIB),
        cost_estimate=cost(2 * count * tokens * width * 4, 5 * count * width),
        name="pack_rows",
    )(
        place,
        by_even,
        by_odd,
        fresh,
        turn,
        gain_row,
        front_table,
        back_table,
        slot_shares,
    )
    rows = exchanged(packed)
    (w_gate,) = loaded(rows[len(rows) * 3 // 8], w_gate[0])
    back_rows = split(back_pairs, packed[0])
    chunk, tile = min(256, units), width // 7
    grads, rows_t, hidden_t, dgate, dup, *parts = pl.pallas_call(
        functools.partial(expert_kernel, chunk, tile, pieces, halves),
        out_shape=(
            held((count, width)),
            held((width, count)),
            held((units, count)),
            held((count, units)),
            held((count, units)),
        )
        + (shape((count // halves, 2 * width)),) * halves,
        in_specs=[whole()] * (3 + pieces + halves),
        out_specs=(whole(),) * (5 + halves),
        scratch_shapes=[
            pltpu.VMEM((2 * count, width), BF16),
            pltpu.VMEM((width, count), BF16),
            pltpu.VMEM((units, count), BF16),
            pltpu.VMEM((units, count), BF16),
            pltpu.VMEM((count, units), BF16),
        ],
        compiler_params=pltpu.CompilerParams(vmem_limit_bytes=(6 if count <= 128 else 32) * MIB),
        cost_estimate=cost(2 * count * width * units * 8, 6 * width * units),
        name="expert_rows",
    )(w_gate, w_up[0], w_down[0], *rows, *back_rows)
    neighbour = swapped(parts)
    (out_gate,) = weight_grads(parts[0], (mirror_gate[0],), (rows_t,), (dgate,), (True,))
    back = exchanged(merged(neighbour), 2)
    out_up, out_down = weight_grads(
        back[0], (mirror_up[0], mirror_down[0]), (rows_t, hidden_t), (dup, grads), (True, False)
    )
    forward_out, grad_input = pl.pallas_call(
        combine_kernel,
        out_shape=(shape((tokens, width)), shape((tokens, width))),
        in_specs=[whole()] * (7 + pairs),
        out_specs=(whole(),) * 2,
        compiler_params=pltpu.CompilerParams(vmem_limit_bytes=6 * MIB),
        cost_estimate=cost(2 * count * tokens * width * 3, 4 * count * width),
        name="combine_rows",
    )(front, upstream, saved, gain_row, front_picks, front_shares, back_picks, *(back[i] for i in ((0, 3, 1, 2) if pairs == 4 else (0,))))
    return (forward_out[None], grad_input[None], out_gate[None], out_up[None], out_down[None])


def solution(mesh):
    return jax.shard_map(
        body,
        mesh=mesh,
        in_specs=(
            P("ep", None),
            P("section", "ep", None),
            P("section", "ep", None),
            P("ep", None),
            P("section", "ep", None),
            P("section", None),
            P("section", "ep", None),
            P("section", "ep", None),
            P("section", "ep", None),
            P("section", "ep", None),
            P("section", None, "ep"),
            P("section", None, "ep"),
            P("section", "ep", None),
            P("section", None, "ep"),
            P("section", None, "ep"),
            P("section", "ep", None),
        ),
        out_specs=(
            P("section", "ep", None),
            P("section", "ep", None),
            P("section", None, "ep"),
            P("section", None, "ep"),
            P("section", "ep", None),
        ),
        check_vma=False,
    )
```
